128 devices in a mesh: row: 8 (over x, core), col: 16 (over z, y).
Axes of the slice: x: 4, y: 4, z: 4, core: 2. Of those that a mesh axis runs over, the one named last changes fastest.
Arguments:
- matrix: bfloat16 [16384, 16384], P('row', 'col'), may hold values from -6 to 6
- inverses: bfloat16 [2, 512, 512], replicated, may hold values from -0.01171875 to 0.01171875
- adjoint: bfloat16 [64, 16384], P(None, 'col'), may hold values from -0.046875 to 0.046875
- focal_nodes: int32 [64], replicated, may hold values from 0 to 16383
- adjacency: int32 [4, 16384], P(None, ('row', 'col')), may hold values from 0 to 127
- conductance: float32 [4, 16384], P(None, ('row', 'col')), may hold values from 0.25 to 1
Outputs:
- trailing: bfloat16 [16384, 16384], P('row', 'col')
- currents: float32 [64, 16384], P(None, ('row', 'col'))
The draws below stay inside these ranges and needn't reach their ends.
Inputs may be any that keep to these rules, and one draw needn't show every extreme that they name: `focal_nodes`: each entry is a node index. `adjacency`: each entry is an index within the neighbouring tile.
All inputs are finite; a program needn't handle non-finite values.
Results may differ from the reference program's by a relative error of at most 0.0065.
Values may be sent and summed in bfloat16 or wider, within the bound.
No kernel may reach another device: no remote copies, remote signals or barrier semaphores. Data moves between devices by JAX's collectives and lax.ppermute only.
A program may use at most 64 MiB of HBM per device.

```python
import math
import jax
import jax.numpy as jnp

ORDER = 16384
PANEL = 512
SOURCES = 64
TILE_NODES = 128
N_ROW = 8
N_COL = 16


def touch_ends(entries, stream_key, least, high):
    shape = entries.shape
    spot = [jax.random.randint(jax.random.fold_in(stream_key, axis), (), 0, shape[axis]) for axis in range(len(shape))]
    entries = entries.at[tuple(spot)].set(least)
    longest = shape.index(max(shape))
    spot[longest] = (spot[longest] + 1) % shape[longest]
    return entries.at[tuple(spot)].set(high)


def shard_levels(stream_key, shape, pieces, least, largest):
    def one(axis_at, parts):
        steps = jax.random.uniform(jax.random.fold_in(jax.random.fold_in(stream_key, 6), axis_at), (parts,), jnp.float32, least / len(pieces), largest / len(pieces))
        return jnp.repeat(jnp.exp(steps), shape[axis_at] // parts).reshape((-1,) + (1,) * (len(shape) - axis_at - 1))

    loudness = one(*pieces[0])
    for cut in pieces[1:]:
        loudness = loudness * one(*cut)
    return loudness


def gaussian(own_key, dims, deviation, most, shards=(), dtype=jnp.bfloat16):
    result = deviation * jax.random.normal(own_key, dims, jnp.float32)
    if shards:
        result = result * shard_levels(own_key, dims, shards, -0.22, 0.18)
    return jnp.clip(result, -most, most).astype(dtype)


def setup_inputs(seed: int = 0) -> dict:
    arg_keys = jax.random.split(jax.random.key(seed), 7)
    return {
        "matrix": gaussian(arg_keys[0], (ORDER, ORDER), 1.0, 6.0, ((0, 8), (1, 16))),
        "inverses": gaussian(arg_keys[1], (2, PANEL, PANEL), (PANEL * PANEL) ** -0.5, 0.01171875),
        "adjoint": gaussian(arg_keys[2], (SOURCES, ORDER), ORDER ** -0.5, 0.046875, ((1, 16),)),
        "focal_nodes": touch_ends(jax.random.randint(arg_keys[3], (SOURCES,), 0, ORDER), jax.random.fold_in(arg_keys[3], 1), 0, ORDER - 1).astype(jnp.int32),
        "adjacency": touch_ends(jax.random.randint(arg_keys[4], (4, ORDER), 0, TILE_NODES), jax.random.fold_in(arg_keys[4], 1), 0, TILE_NODES - 1).astype(jnp.int32),
        "conductance": jnp.clip(jnp.exp(math.log(1.0) - 1.3862944 * jax.random.uniform(arg_keys[5], (4, ORDER), jnp.float32) ** shard_levels(arg_keys[5], (4, ORDER), ((1, 128),), -0.2, 0.2)), 0.25, 1.0),
    }


def reference(matrix, inverses, adjoint, focal_nodes, adjacency, conductance):
    panel_width = inverses.shape[1]
    current = matrix
    for which in range(2):
        offset = which * panel_width
        columns = current[:, offset:offset + panel_width]
        upper_rows = current[offset:offset + panel_width, :]
        lower_part = jnp.dot(columns, inverses[which], preferred_element_type=jnp.float32).astype(jnp.bfloat16)
        current = (current.astype(jnp.float32) - jnp.dot(lower_part, upper_rows, preferred_element_type=jnp.float32)).astype(jnp.bfloat16)
    trailing = current
    sources = adjoint.shape[0]
    tile_nodes = ORDER // (N_ROW * N_COL)
    injected = jnp.dot(adjoint, trailing.T, preferred_element_type=jnp.float32)
    injected = injected + trailing[:, focal_nodes].T.astype(jnp.float32)
    tile_grid = injected.reshape(sources, N_ROW, N_COL, tile_nodes)
    padded = jnp.pad(tile_grid, ((0, 0), (1, 1), (1, 1), (0, 0)))
    neighbours = jnp.stack([padded[:, :-2, 1:-1], padded[:, 2:, 1:-1], padded[:, 1:-1, :-2], padded[:, 1:-1, 2:]])
    links = jnp.broadcast_to(adjacency.reshape(4, 1, N_ROW, N_COL, tile_nodes), neighbours.shape)
    gathered = jnp.take_along_axis(neighbours, links, axis=4)
    weights = conductance.reshape(4, 1, N_ROW, N_COL, tile_nodes)
    currents = tile_grid - jnp.sum(weights * gathered, axis=0)
    return trailing, currents.reshape(sources, ORDER)
```

```python
import functools

import jax
import jax.numpy as jnp
from jax import lax
from jax.experimental import pallas as pl
from jax.experimental.pallas import tpu as pltpu
from jax.sharding import PartitionSpec as P

BF16 = jnp.bfloat16
F32 = jnp.float32


def multiply(left, right):
    return jnp.dot(left, right, preferred_element_type=F32)


def spread_rows(value, row):
    away = [lax.ppermute(value, "row", [(0, at)]) for at in (2, 6, 4)]
    even = jnp.where(row == 0, value, away[0] + away[1] + away[2])
    other = lax.ppermute(even, "row", [(at, at + 1) for at in range(0, 8, 2)])
    return jnp.where(row % 2 == 0, even, other)


def scatter_cols(pieces, col):
    count = pieces.shape[0]
    got = jnp.where(col == 0, pieces[0], jnp.zeros_like(pieces[0]))
    for at in range(1, count):
        got = got + lax.ppermute(pieces[at], "col", [(0, at)])
    return got


def update_kernel(base_ref, low_ref, up0_ref, up1_ref, stacked_ref, out_ref, part_ref):
    half = up0_ref.shape[0]
    sources = part_ref.shape[0]
    low = low_ref[0]
    lifted = multiply(low[:, :half], up0_ref[...]) + multiply(low[:, half:], up1_ref[...])
    done = (base_ref[...].astype(F32) - lifted).astype(BF16)
    out_ref[...] = done
    product = lax.dot_general(
        stacked_ref[...], done, (((1,), (1,)), ((), ())), preferred_element_type=F32
    )
    part_ref[...] = product[:sources] + product[sources:]


def update(base, low, up0, up1, stacked):
    tiles = low.shape[0]
    rows, width = base.shape
    step = rows // tiles
    depth = low.shape[2]
    sources = stacked.shape[0] // 2
    whole = lambda i: (0, 0)
    return pl.pallas_call(
        update_kernel,
        grid=(tiles,),
        in_specs=[
            pl.BlockSpec((step, width), lambda i: (i, 0)),
            pl.BlockSpec((1, step, depth), lambda i: (i, 0, 0)),
            pl.BlockSpec(up0.shape, whole),
            pl.BlockSpec(up1.shape, whole),
            pl.BlockSpec(stacked.shape, whole),
        ],
        out_specs=[
            pl.BlockSpec((step, width), lambda i: (i, 0)),
            pl.BlockSpec((sources, step), lambda i: (0, i)),
        ],
        out_shape=[
            jax.ShapeDtypeStruct((rows, width), BF16),
            jax.ShapeDtypeStruct((sources, rows), F32),
        ],
        compiler_params=pltpu.CompilerParams(vmem_limit_bytes=32 << 20),
    )(base, low, up0, up1, stacked)


def shards(matrix, inverses, adjoint, focal_nodes, adjacency, conductance):
    row, col = lax.axis_index("row"), lax.axis_index("col")
    cols = lax.axis_size("col")
    panel = inverses.shape[1]
    both = 2 * panel
    sources = adjoint.shape[0]
    rows_here, width_here = matrix.shape

    panels = matrix[:, :both]
    upper = matrix[:both]
    corner01 = spread_rows(upper[:panel, panel:both], row)
    corner10 = spread_rows(upper[panel:, :panel], row)
    up0 = spread_rows(upper[:panel], row)
    up1 = spread_rows(upper[panel:], row)

    low0 = multiply(panels[:, :panel], inverses[0]).astype(BF16)
    piece0 = scatter_cols(low0.reshape(cols, -1, panel), col)

    second = (panels[:, panel:].astype(F32) - multiply(low0, corner01)).astype(BF16)
    low1 = multiply(second, inverses[1]).astype(BF16)
    cross = multiply(corner10, inverses[0]).astype(BF16)
    joined = jnp.concatenate([low1.reshape(cols, -1, panel), cross.reshape(cols, -1, panel)], axis=1)
    piece1 = scatter_cols(joined, col)

    tile = rows_here // cols
    share = panel // cols // 2
    cross_piece = jnp.concatenate([piece1[tile : tile + share], piece1[tile + share :]], axis=1)
    piece = jnp.concatenate(
        [jnp.concatenate([piece0, piece1[:tile]], axis=1), cross_piece], axis=0
    )
    low = lax.all_gather(piece, "col")
    crossed = low[:, tile:]
    cross_all = jnp.stack([crossed[:, :, :panel], crossed[:, :, panel:]], axis=1).reshape(panel, panel)
    up1 = (up1.astype(F32) - multiply(cross_all, up0)).astype(BF16)

    positions = col * width_here + lax.broadcasted_iota(jnp.int32, (sources, width_here), 1)
    onehot = (positions == focal_nodes[:, None]).astype(BF16)
    stacked = jnp.concatenate([adjoint, onehot], axis=0)
    trailing, partial_sum = update(matrix, low, up0, up1, stacked)

    swapped = lax.all_to_all(
        partial_sum.reshape(sources, cols, tile), "col", split_axis=1, concat_axis=0, tiled=True
    )
    injected = jnp.sum(swapped.reshape(cols, sources, tile), axis=0)

    count_row = lax.axis_size("row")
    neighbours = jnp.stack(
        [
            lax.ppermute(injected, "row", [(i, i + 1) for i in range(count_row - 1)]),
            lax.ppermute(injected, "row", [(i + 1, i) for i in range(count_row - 1)]),
            lax.ppermute(injected, "col", [(i, i + 1) for i in range(cols - 1)]),
            lax.ppermute(injected, "col", [(i + 1, i) for i in range(cols - 1)]),
        ]
    )
    node_ids = lax.broadcasted_iota(jnp.int32, (1, 1, tile), 2)
    selector = (adjacency[:, :, None] == node_ids).astype(F32)
    gathered = jnp.einsum("ksj,kij->ksi", neighbours, selector, precision=lax.Precision.HIGHEST)
    currents = injected - jnp.sum(conductance[:, None, :] * gathered, axis=0)
    return (trailing, currents)


def solution(mesh):
    placed = (
        P("row", "col"),
        P(),
        P(None, "col"),
        P(),
        P(None, ("row", "col")),
        P(None, ("row", "col")),
    )
    return jax.shard_map(
        shards,
        mesh=mesh,
        in_specs=placed,
        out_specs=(P("row", "col"), P(None, ("row", "col"))),
        check_vma=False,
    )
```

```python
import jax
import jax.numpy as jnp
from jax import lax
from jax.experimental import pallas as pl
from jax.experimental.pallas import tpu as pltpu
from jax.sharding import PartitionSpec as P

BF16 = jnp.bfloat16
F32 = jnp.float32


def multiply(left, right):
    return jnp.dot(left, right, preferred_element_type=F32)


def send(value, axis, pairs):
    return lax.ppermute(value, axis, pairs)


def along_x(value):
    return [send(value, "row", [(0, at)]) for at in (4, 2, 6)]


def on_even(value, got, row):
    return jnp.where(row == 0, value, got[0] + got[1] + got[2])


def gather_first_half(value, col):
    for bit in (1, 2, 4):
        other = send(value, "col", [(at, at ^ bit) for at in range(16)])
        after = (col & bit) == 0
        value = jnp.concatenate(
            [jnp.where(after, value, other), jnp.where(after, other, value)], axis=0
        )
    return jnp.where(col < 8, value, send(value, "col", [(at, at + 8) for at in range(8)]))


def hop_near(value):
    return send(value, "row", [(0, 2)]) + send(value, "row", [(0, 6)])


def hop_far(value, near, row):
    half = value.shape[0] // 2
    far = [send(near[:half], "row", [(2, 4)]), send(near[half:], "row", [(6, 4)])]
    return jnp.where(row == 0, value, near + jnp.concatenate(far, axis=0))


def to_odd(value):
    return send(value, "row", [(at, at + 1) for at in range(0, 8, 2)])


REGIONS = ((1, 5, 13, 2), (3, 7, 15, 0), (4, 8, 6, 9), (12, 14, 11, 10))


def lift_kernel(table_ref, *refs):
    tiles, (mixed_ref, inverses_ref), outs = refs[:4], refs[4:6], refs[6:]
    panel = inverses_ref.shape[1]
    rows = jnp.concatenate([tile_ref[...] for tile_ref in tiles], axis=0)
    first, second = inverses_ref[0], inverses_ref[1]
    cross = multiply(mixed_ref[:panel], first).astype(BF16)
    low0 = multiply(rows[:, :panel], first).astype(BF16)
    low1 = rows[:, panel:].astype(F32) - multiply(low0, mixed_ref[panel:])
    low1 = multiply(low1.astype(BF16), second).astype(BF16)
    low0 = (low0.astype(F32) - multiply(low1, cross)).astype(BF16)
    done = jnp.concatenate([low0, low1], axis=1)
    for which, out_ref in enumerate(outs):

        @pl.when(pl.program_id(0) == which)
        def _(out_ref=out_ref):
            out_ref[...] = done


def lift(panels, mixed, inverses, tile):
    depth = inverses.shape[0] * inverses.shape[1]
    table = jnp.array([at for members in REGIONS for at in members], dtype=jnp.int32)
    bundle = jax.ShapeDtypeStruct((4 * tile, depth), BF16)
    return pl.pallas_call(
        lift_kernel,
        grid_spec=pltpu.PrefetchScalarGridSpec(
            num_scalar_prefetch=1,
            grid=(4,),
            in_specs=[
                pl.BlockSpec((tile, depth), lambda i, table, j=j: (table[4 * i + j], 0))
                for j in range(4)
            ]
            + [
                pl.BlockSpec(mixed.shape, lambda i, table: (0, 0)),
                pl.BlockSpec(inverses.shape, lambda i, table: (0, 0, 0)),
            ],
            out_specs=[pl.BlockSpec(bundle.shape, lambda i, table: (0, 0)) for _ in REGIONS],
        ),
        out_shape=[bundle] * 4,
        compiler_params=pltpu.CompilerParams(vmem_limit_bytes=40 << 20),
    )(table, *([panels] * 4), mixed, inverses)


def pass_on(bundles, col, tile):
    own = bundles[1][3 * tile :]
    got = [send(bundle, "col", [(0, members[0])]) for bundle, members in zip(bundles, REGIONS)]
    got = got[0] + got[1] + got[2] + got[3]
    piece = jnp.where(col == 0, own, got[:tile])
    for j in range(1, 4):
        part = got[j * tile : (j + 1) * tile]
        piece = piece + send(part, "col", [(m[0], m[j]) for m in REGIONS if m[j] != 0])
    return piece


def adjoint_kernel(raw_ref, parts_ref, piece_ref, out_ref):
    sources, tile = raw_ref.shape
    total = raw_ref[...]
    for k in range(parts_ref.shape[0] // sources):
        total = total - lax.dot_general(
            parts_ref[k * sources : (k + 1) * sources],
            piece_ref[:, k * tile : (k + 1) * tile].astype(F32),
            (((1,), (1,)), ((), ())),
            precision=lax.Precision.HIGHEST,
            preferred_element_type=F32,
        )
    out_ref[...] = total


def update_kernel(base_ref, low_ref, mixed_ref, plain_ref, out_ref, up_ref):
    rows, width = base_ref.shape
    half = up_ref.shape[0] // 2

    @pl.when(pl.program_id(0) == 0)
    def _():
        up_ref[:half, :half] = plain_ref[:half]
        up_ref[:half, half:] = mixed_ref[half:]
        up_ref[half:, :half] = mixed_ref[:half]
        up_ref[half:, half:] = plain_ref[half:]

    low = low_ref[...].reshape(rows, up_ref.shape[0])
    out_ref[...] = (base_ref[...].astype(F32) - multiply(low, up_ref[...])).astype(BF16)


def update(base, low, mixed, plain):
    rows, width = base.shape
    tiles, tile, depth = low.shape
    group = 4
    step = group * tile
    return pl.pallas_call(
        update_kernel,
        grid=(rows // step,),
        in_specs=[
            pl.BlockSpec((step, width), lambda i: (i, 0)),
            pl.BlockSpec((group, tile, depth), lambda i: (i, 0, 0)),
            pl.BlockSpec(mixed.shape, lambda i: (0, 0)),
            pl.BlockSpec(plain.shape, lambda i: (0, 0)),
        ],
        out_specs=pl.BlockSpec((step, width), lambda i: (i, 0)),
        out_shape=jax.ShapeDtypeStruct((rows, width), BF16),
        scratch_shapes=[pltpu.VMEM((depth, width), BF16)],
        compiler_params=pltpu.CompilerParams(vmem_limit_bytes=56 << 20),
    )(base, low, mixed, plain)


def shards(matrix, inverses, adjoint, focal_nodes, adjacency, conductance):
    row, col = lax.axis_index("row"), lax.axis_index("col")
    rows_axis, cols = lax.axis_size("row"), lax.axis_size("col")
    panel = inverses.shape[1]
    both = 2 * panel
    sources = adjoint.shape[0]
    rows_here, width_here = matrix.shape
    tile = rows_here // cols
    even = row % 2 == 0

    mixed = jnp.concatenate([matrix[panel:both, :panel], matrix[:panel, panel:both]], axis=0)
    upper_half = lax.broadcasted_iota(jnp.int32, (both, panel), 0) < panel
    plain = jnp.where(upper_half, matrix[:both, :panel], matrix[:both, panel:both])

    mixed = hop_far(mixed, hop_near(mixed), row)
    mixed = jnp.where(even, mixed, to_odd(mixed))
    positions = col * width_here + lax.broadcasted_iota(jnp.int32, (sources, width_here), 1)
    onehot = (positions == focal_nodes[:, None]).astype(BF16)
    stacked = jnp.concatenate([adjoint, onehot], axis=0)
    product = lax.dot_general(
        stacked, matrix, (((1,), (1,)), ((), ())), preferred_element_type=F32
    )
    raw = product[:sources] + product[sources:]
    mixed, raw, plain = lax.optimization_barrier((mixed, raw, plain))

    bundles = lift(matrix, mixed, inverses, tile)
    bundles, raw = lax.optimization_barrier((bundles, raw))
    swapped = lax.all_to_all(
        raw.reshape(sources, cols, tile), "col", split_axis=1, concat_axis=0, tiled=True
    )
    raw_tile = jnp.sum(swapped.reshape(cols, sources, tile), axis=0)
    piece = pass_on(bundles, col, tile)
    piece, raw_tile, plain = lax.optimization_barrier((piece, raw_tile, plain))
    low = lax.all_gather(piece, "col")
    parts = gather_first_half(raw_tile, col)

    parts = on_even(parts, along_x(parts), row)
    parts = jnp.where(even, parts, to_odd(parts))
    plain = on_even(plain, along_x(plain), row)
    plain = jnp.where(even, plain, to_odd(plain))
    parts, plain = lax.optimization_barrier((parts, plain))
    trailing = update(matrix, low, mixed, plain)
    injected = pl.pallas_call(
        adjoint_kernel, out_shape=jax.ShapeDtypeStruct((sources, tile), F32)
    )(raw_tile, parts, piece)

    neighbours = (
        [
            send(injected, "row", [(i, i + 1) for i in range(rows_axis - 1)]),
            send(injected, "row", [(i + 1, i) for i in range(rows_axis - 1)]),
            send(injected, "col", [(i, i + 1) for i in range(cols - 1)]),
            send(injected, "col", [(i + 1, i) for i in range(cols - 1)]),
        ]
    )
    neighbours, trailing = lax.optimization_barrier((neighbours, trailing))
    neighbours = jnp.stack(neighbours)
    node_ids = lax.broadcasted_iota(jnp.int32, (1, 1, tile), 2)
    selector = (adjacency[:, :, None] == node_ids).astype(F32)
    gathered = jnp.einsum("ksj,kij->ksi", neighbours, selector, precision=lax.Precision.HIGHEST)
    currents = injected - jnp.sum(conductance[:, None, :] * gathered, axis=0)
    return (trailing, currents)


def solution(mesh):
    placed = (
        P("row", "col"),
        P(),
        P(None, "col"),
        P(),
        P(None, ("row", "col")),
        P(None, ("row", "col")),
    )
    return jax.shard_map(
        shards,
        mesh=mesh,
        in_specs=placed,
        out_specs=(P("row", "col"), P(None, ("row", "col"))),
        check_vma=False,
    )
```

```python
import jax
import jax.numpy as jnp
from jax import lax
from jax.experimental import pallas as pl
from jax.experimental.pallas import tpu as pltpu
from jax.sharding import PartitionSpec as P

BF16 = jnp.bfloat16
F32 = jnp.float32


def multiply(left, right):
    return jnp.dot(left, right, preferred_element_type=F32)


def send(value, axis, pairs):
    return lax.ppermute(value, axis, pairs)


def along_x(value):
    return [send(value, "row", [(0, at)]) for at in (4, 2, 6)]


def on_even(value, got, row):
    return jnp.where(row == 0, value, got[0] + got[1] + got[2])


def gather_first_half(value, col):
    for bit in (1, 2, 4):
        other = send(value, "col", [(at, at ^ bit) for at in range(16)])
        after = (col & bit) == 0
        value = jnp.concatenate(
            [jnp.where(after, value, other), jnp.where(after, other, value)], axis=0
        )
    return jnp.where(col < 8, value, send(value, "col", [(at, at + 8) for at in range(8)]))


def to_odd(value):
    return send(value, "row", [(at, at + 1) for at in range(0, 8, 2)])


REGIONS = ((1, 5, 13, 2), (3, 7, 15, 0), (4, 8, 6, 9), (12, 14, 11, 10))


def lift_kernel(table_ref, *refs):
    tiles, (mixed_ref, inverses_ref), outs = refs[:4], refs[4:6], refs[6:]
    panel = inverses_ref.shape[1]
    rows = jnp.concatenate([tile_ref[...] for tile_ref in tiles], axis=0)
    first, second = inverses_ref[0], inverses_ref[1]
    cross = multiply(mixed_ref[:panel], first).astype(BF16)
    low0 = multiply(rows[:, :panel], first).astype(BF16)
    low1 = rows[:, panel:].astype(F32) - multiply(low0, mixed_ref[panel:])
    low1 = multiply(low1.astype(BF16), second).astype(BF16)
    low0 = (low0.astype(F32) - multiply(low1, cross)).astype(BF16)
    done = jnp.concatenate([low0, low1], axis=1)
    for which, out_ref in enumerate(outs):

        @pl.when(pl.program_id(0) == which)
        def _(out_ref=out_ref):
            out_ref[...] = done


def lift(panels, mixed, inverses, tile):
    depth = inverses.shape[0] * inverses.shape[1]
    table = jnp.array([at for members in REGIONS for at in members], dtype=jnp.int32)
    bundle = jax.ShapeDtypeStruct((4 * tile, depth), BF16)
    return pl.pallas_call(
        lift_kernel,
        grid_spec=pltpu.PrefetchScalarGridSpec(
            num_scalar_prefetch=1,
            grid=(4,),
            in_specs=[
                pl.BlockSpec((tile, depth), lambda i, table, j=j: (table[4 * i + j], 0))
                for j in range(4)
            ]
            + [
                pl.BlockSpec(mixed.shape, lambda i, table: (0, 0)),
                pl.BlockSpec(inverses.shape, lambda i, table: (0, 0, 0)),
            ],
            out_specs=[pl.BlockSpec(bundle.shape, lambda i, table: (0, 0)) for _ in REGIONS],
        ),
        out_shape=[bundle] * 4,
        compiler_params=pltpu.CompilerParams(vmem_limit_bytes=40 << 20),
    )(table, *([panels] * 4), mixed, inverses)


def pass_on(bundles, col, tile):
    own = bundles[1][3 * tile :]
    got = [send(bundle, "col", [(0, members[0])]) for bundle, members in zip(bundles, REGIONS)]
    got = got[0] + got[1] + got[2] + got[3]
    piece = jnp.where(col == 0, own, got[:tile])
    for j in range(1, 4):
        part = got[j * tile : (j + 1) * tile]
        piece = piece + send(part, "col", [(m[0], m[j]) for m in REGIONS if m[j] != 0])
    return piece


def adjoint_kernel(raw_ref, parts_ref, piece_ref, out_ref):
    sources, tile = raw_ref.shape
    total = raw_ref[...]
    for k in range(parts_ref.shape[0] // sources):
        total = total - lax.dot_general(
            parts_ref[k * sources : (k + 1) * sources],
            piece_ref[:, k * tile : (k + 1) * tile].astype(F32),
            (((1,), (1,)), ((), ())),
            precision=lax.Precision.HIGHEST,
            preferred_element_type=F32,
        )
    out_ref[...] = total


def update_kernel(base_ref, low_ref, mixed_ref, plain_ref, out_ref, up_ref):
    rows, width = base_ref.shape
    half = up_ref.shape[0] // 2

    @pl.when(pl.program_id(0) == 0)
    def _():
        up_ref[:half, :half] = plain_ref[:half]
        up_ref[:half, half:] = mixed_ref[half:]
        up_ref[half:, :half] = mixed_ref[:half]
        up_ref[half:, half:] = plain_ref[half:]

    low = low_ref[...].reshape(rows, up_ref.shape[0])
    out_ref[...] = (base_ref[...].astype(F32) - multiply(low, up_ref[...])).astype(BF16)


def update(base, low, mixed, plain):
    rows, width = base.shape
    tiles, tile, depth = low.shape
    group = 4
    step = group * tile
    return pl.pallas_call(
        update_kernel,
        grid=(rows // step,),
        in_specs=[
            pl.BlockSpec((step, width), lambda i: (i, 0)),
            pl.BlockSpec((group, tile, depth), lambda i: (i, 0, 0)),
            pl.BlockSpec(mixed.shape, lambda i: (0, 0)),
            pl.BlockSpec(plain.shape, lambda i: (0, 0)),
        ],
        out_specs=pl.BlockSpec((step, width), lambda i: (i, 0)),
        out_shape=jax.ShapeDtypeStruct((rows, width), BF16),
        scratch_shapes=[pltpu.VMEM((depth, width), BF16)],
        compiler_params=pltpu.CompilerParams(vmem_limit_bytes=56 << 20),
    )(base, low, mixed, plain)


def shards(matrix, inverses, adjoint, focal_nodes, adjacency, conductance):
    row, col = lax.axis_index("row"), lax.axis_index("col")
    rows_axis, cols = lax.axis_size("row"), lax.axis_size("col")
    panel = inverses.shape[1]
    both = 2 * panel
    sources = adjoint.shape[0]
    rows_here, width_here = matrix.shape
    tile = rows_here // cols
    even = row % 2 == 0

    mixed = jnp.concatenate([matrix[panel:both, :panel], matrix[:panel, panel:both]], axis=0)
    upper_half = lax.broadcasted_iota(jnp.int32, (both, panel), 0) < panel
    plain = jnp.where(upper_half, matrix[:both, :panel], matrix[:both, panel:both])

    mixed_lines = along_x(mixed)
    positions = col * width_here + lax.broadcasted_iota(jnp.int32, (sources, width_here), 1)
    onehot = (positions == focal_nodes[:, None]).astype(BF16)
    stacked = jnp.concatenate([adjoint, onehot], axis=0)
    product = lax.dot_general(
        stacked, matrix, (((1,), (1,)), ((), ())), preferred_element_type=F32
    )
    raw = (product[:sources] + product[sources:]).astype(BF16)
    swapped = lax.all_to_all(
        raw.reshape(sources, cols, tile), "col", split_axis=1, concat_axis=0, tiled=True
    )
    raw_tile = jnp.sum(swapped.reshape(cols, sources, tile).astype(F32), axis=0)
    mixed_lines, raw_tile = lax.optimization_barrier((mixed_lines, raw_tile))
    mixed = on_even(mixed, mixed_lines, row)
    mixed = jnp.where(even, mixed, to_odd(mixed))

    bundles = lift(matrix, mixed, inverses, tile)
    bundles, raw_tile = lax.optimization_barrier((bundles, raw_tile))
    parts = gather_first_half(raw_tile, col)
    piece = pass_on(bundles, col, tile)
    piece, plain = lax.optimization_barrier((piece, plain))
    low = lax.all_gather(piece, "col")

    parts = on_even(parts, along_x(parts), row)
    parts = jnp.where(even, parts, to_odd(parts))
    plain = on_even(plain, along_x(plain), row)
    plain = jnp.where(even, plain, to_odd(plain))
    parts, plain = lax.optimization_barrier((parts, plain))
    trailing = update(matrix, low, mixed, plain)
    injected = pl.pallas_call(
        adjoint_kernel, out_shape=jax.ShapeDtypeStruct((sources, tile), F32)
    )(raw_tile, parts, piece)

    neighbours = (
        [
            send(injected, "row", [(i, i + 1) for i in range(rows_axis - 1)]),
            send(injected, "row", [(i + 1, i) for i in range(rows_axis - 1)]),
            send(injected, "col", [(i, i + 1) for i in range(cols - 1)]),
            send(injected, "col", [(i + 1, i) for i in range(cols - 1)]),
        ]
    )
    neighbours, trailing = lax.optimization_barrier((neighbours, trailing))
    neighbours = jnp.stack(neighbours)
    node_ids = lax.broadcasted_iota(jnp.int32, (1, 1, tile), 2)
    selector = (adjacency[:, :, None] == node_ids).astype(F32)
    gathered = jnp.einsum("ksj,kij->ksi", neighbours, selector, precision=lax.Precision.HIGHEST)
    currents = injected - jnp.sum(conductance[:, None, :] * gathered, axis=0)
    return (trailing, currents)


def solution(mesh):
    placed = (
        P("row", "col"),
        P(),
        P(None, "col"),
        P(),
        P(None, ("row", "col")),
        P(None, ("row", "col")),
    )
    return jax.shard_map(
        shards,
        mesh=mesh,
        in_specs=placed,
        out_specs=(P("row", "col"), P(None, ("row", "col"))),
        check_vma=False,
    )
```

```python
import jax
import jax.numpy as jnp
from jax import lax
from jax.experimental import pallas as pl
from jax.experimental.pallas import tpu as pltpu
from jax.sharding import PartitionSpec as P

BF16 = jnp.bfloat16
F32 = jnp.float32


def multiply(left, right):
    return jnp.dot(left, right, preferred_element_type=F32)


def send(value, axis, pairs):
    return lax.ppermute(value, axis, pairs)


def along_x(value):
    return [send(value, "row", [(0, at)]) for at in (4, 2, 6)]


def on_even(value, got, row):
    return jnp.where(row == 0, value, got[0] + got[1] + got[2])


def exchange(value, col, bit):
    other = send(value, "col", [(at, at ^ bit) for at in range(16)])
    after = (col & bit) == 0
    return jnp.concatenate(
        [jnp.where(after, value, other), jnp.where(after, other, value)], axis=0
    )


def gather_first_half(value, col):
    value = exchange(exchange(value, col, 2), col, 4)
    return jnp.where(col < 8, value, send(value, "col", [(at, at + 8) for at in range(8)]))


def to_odd(value):
    return send(value, "row", [(at, at + 1) for at in range(0, 8, 2)])


REGIONS = ((1, 5, 13, 2), (3, 7, 15, 0), (4, 8, 6, 9), (12, 14, 11, 10))


def lift_kernel(table_ref, *refs):
    lows, tiles, (mixed_ref, inverses_ref), outs = refs[:4], refs[4:8], refs[8:10], refs[10:14]
    cross_ref = refs[14]
    panel = inverses_ref.shape[1]

    @pl.when(pl.program_id(0) == 0)
    def _():
        cross_ref[...] = multiply(mixed_ref[:panel], inverses_ref[0]).astype(BF16)

    low0 = jnp.concatenate([low_ref[...] for low_ref in lows], axis=0)
    rows = jnp.concatenate([tile_ref[...] for tile_ref in tiles], axis=0)
    low1 = rows.astype(F32) - multiply(low0, mixed_ref[panel:])
    low1 = multiply(low1.astype(BF16), inverses_ref[1]).astype(BF16)
    low0 = (low0.astype(F32) - multiply(low1, cross_ref[...])).astype(BF16)
    for which, out_ref in enumerate(outs):

        @pl.when(pl.program_id(0) == which)
        def _(out_ref=out_ref):
            out_ref[:, :panel] = low0
            out_ref[:, panel:] = low1


def lift(low0, panels, mixed, inverses, tile):
    panel = inverses.shape[1]
    table = jnp.array([at for members in REGIONS for at in members], dtype=jnp.int32)
    bundle = jax.ShapeDtypeStruct((4 * tile, 2 * panel), BF16)
    return pl.pallas_call(
        lift_kernel,
        grid_spec=pltpu.PrefetchScalarGridSpec(
            num_scalar_prefetch=1,
            grid=(4,),
            in_specs=[
                pl.BlockSpec((tile, panel), lambda i, table, j=j, at=at: (table[4 * i + j], at))
                for at in range(2)
                for j in range(4)
            ]
            + [
                pl.BlockSpec(mixed.shape, lambda i, table: (0, 0)),
                pl.BlockSpec(inverses.shape, lambda i, table: (0, 0, 0)),
            ],
            out_specs=[pl.BlockSpec(bundle.shape, lambda i, table: (0, 0)) for _ in REGIONS],
            scratch_shapes=[pltpu.VMEM((panel, panel), BF16)],
        ),
        out_shape=[bundle] * 4,
        compiler_params=pltpu.CompilerParams(vmem_limit_bytes=56 << 20),
    )(table, *([low0] * 4), *([panels] * 4), mixed, inverses)


def pass_on(bundles, col, tile):
    own = bundles[1][3 * tile :]
    got = [send(bundle, "col", [(0, members[0])]) for bundle, members in zip(bundles, REGIONS)]
    got = got[0] + got[1] + got[2] + got[3]
    piece = jnp.where(col == 0, own, got[:tile])
    for j in range(1, 4):
        part = got[j * tile : (j + 1) * tile]
        piece = piece + send(part, "col", [(m[0], m[j]) for m in REGIONS if m[j] != 0])
    return piece


def adjoint_kernel(raw_ref, parts_ref, piece_ref, out_ref):
    sources, tile = raw_ref.shape
    total = raw_ref[...]
    for k in range(parts_ref.shape[0] // sources):
        total = total - lax.dot_general(
            parts_ref[k * sources : (k + 1) * sources],
            piece_ref[:, k * tile : (k + 1) * tile].astype(F32),
            (((1,), (1,)), ((), ())),
            precision=lax.Precision.HIGHEST,
            preferred_element_type=F32,
        )
    out_ref[...] = total


def update_kernel(base_ref, low_ref, mixed_ref, plain_ref, out_ref, up_ref):
    rows, width = base_ref.shape
    half = up_ref.shape[0] // 2

    @pl.when(pl.program_id(0) == 0)
    def _():
        up_ref[:half, :half] = plain_ref[:half]
        up_ref[:half, half:] = mixed_ref[half:]
        up_ref[half:, :half] = mixed_ref[:half]
        up_ref[half:, half:] = plain_ref[half:]

    low = low_ref[...].reshape(rows, up_ref.shape[0])
    out_ref[...] = (base_ref[...].astype(F32) - multiply(low, up_ref[...])).astype(BF16)


def update(base, low, mixed, plain):
    rows, width = base.shape
    tiles, tile, depth = low.shape
    group = 8
    step = group * tile
    return pl.pallas_call(
        update_kernel,
        grid=(rows // step,),
        in_specs=[
            pl.BlockSpec((step, width), lambda i: (i, 0)),
            pl.BlockSpec((group, tile, depth), lambda i: (i, 0, 0)),
            pl.BlockSpec(mixed.shape, lambda i: (0, 0)),
            pl.BlockSpec(plain.shape, lambda i: (0, 0)),
        ],
        out_specs=pl.BlockSpec((step, width), lambda i: (i, 0)),
        out_shape=jax.ShapeDtypeStruct((rows, width), BF16),
        scratch_shapes=[pltpu.VMEM((depth, width), BF16)],
        compiler_params=pltpu.CompilerParams(vmem_limit_bytes=56 << 20),
    )(base, low, mixed, plain)


def shards(matrix, inverses, adjoint, focal_nodes, adjacency, conductance):
    row, col = lax.axis_index("row"), lax.axis_index("col")
    rows_axis, cols = lax.axis_size("row"), lax.axis_size("col")
    panel = inverses.shape[1]
    both = 2 * panel
    sources = adjoint.shape[0]
    rows_here, width_here = matrix.shape
    tile = rows_here // cols
    even = row % 2 == 0

    mixed = jnp.concatenate([matrix[panel:both, :panel], matrix[:panel, panel:both]], axis=0)
    upper_half = lax.broadcasted_iota(jnp.int32, (both, panel), 0) < panel
    plain = jnp.where(upper_half, matrix[:both, :panel], matrix[:both, panel:both])

    mixed_lines = along_x(mixed)
    positions = col * width_here + lax.broadcasted_iota(jnp.int32, (sources, width_here), 1)
    onehot = (positions == focal_nodes[:, None]).astype(BF16)
    stacked = jnp.concatenate([adjoint, onehot], axis=0)
    product = lax.dot_general(
        stacked, matrix, (((1,), (1,)), ((), ())), preferred_element_type=F32
    )
    raw = (product[:sources] + product[sources:]).astype(BF16)
    swapped = lax.all_to_all(
        raw.reshape(sources, cols, tile), "col", split_axis=1, concat_axis=0, tiled=True
    )
    raw_tile = jnp.sum(swapped.reshape(cols, sources, tile).astype(F32), axis=0)
    low0 = multiply(matrix[:, :panel], inverses[0]).astype(BF16)
    mixed_lines, raw_tile, low0 = lax.optimization_barrier((mixed_lines, raw_tile, low0))
    mixed = on_even(mixed, mixed_lines, row)
    mixed = jnp.where(even, mixed, to_odd(mixed))

    pair = exchange(raw_tile, col, 1)
    mixed, pair = lax.optimization_barrier((mixed, pair))
    bundles = lift(low0, matrix, mixed, inverses, tile)
    bundles, pair = lax.optimization_barrier((bundles, pair))
    parts = gather_first_half(pair, col)
    piece = pass_on(bundles, col, tile)
    piece, plain = lax.optimization_barrier((piece, plain))
    low = lax.all_gather(piece, "col")

    parts = on_even(parts, along_x(parts), row)
    parts = jnp.where(even, parts, to_odd(parts))
    plain = on_even(plain, along_x(plain), row)
    plain = jnp.where(even, plain, to_odd(plain))
    parts, plain = lax.optimization_barrier((parts, plain))
    trailing = update(matrix, low, mixed, plain)
    injected = pl.pallas_call(
        adjoint_kernel, out_shape=jax.ShapeDtypeStruct((sources, tile), F32)
    )(raw_tile, parts, piece)

    neighbours = (
        [
            send(injected, "row", [(i, i + 1) for i in range(rows_axis - 1)]),
            send(injected, "row", [(i + 1, i) for i in range(rows_axis - 1)]),
            send(injected, "col", [(i, i + 1) for i in range(cols - 1)]),
            send(injected, "col", [(i + 1, i) for i in range(cols - 1)]),
        ]
    )
    neighbours, trailing = lax.optimization_barrier((neighbours, trailing))
    neighbours = jnp.stack(neighbours)
    node_ids = lax.broadcasted_iota(jnp.int32, (1, 1, tile), 2)
    selector = (adjacency[:, :, None] == node_ids).astype(F32)
    gathered = jnp.einsum("ksj,kij->ksi", neighbours, selector, precision=lax.Precision.HIGHEST)
    currents = injected - jnp.sum(conductance[:, None, :] * gathered, axis=0)
    return (trailing, currents)


def solution(mesh):
    placed = (
        P("row", "col"),
        P(),
        P(None, "col"),
        P(),
        P(None, ("row", "col")),
        P(None, ("row", "col")),
    )
    return jax.shard_map(
        shards,
        mesh=mesh,
        in_specs=placed,
        out_specs=(P("row", "col"), P(None, ("row", "col"))),
        check_vma=False,
    )
```
